128 devices in a mesh: section: 2 (over y_hi), row: 16 (over x, z), col: 4 (over y_lo, core).
Axes of the slice: x: 4, y: 4 (y_hi: 2, y_lo: 2; y = y_hi * 2 + y_lo), z: 4, core: 2. Of those that a mesh axis runs over, the one named last changes fastest.
Arguments:
- layer_input: bfloat16 [2, 16, 577, 1024], P('section', 'row', None, 'col'), may hold values from -6 to 6
- cotangent: bfloat16 [2, 16, 577, 1024], P('section', 'row', None, 'col'), may hold values from -6 to 6
- norm1_gain: bfloat16 [2, 1024], P('section', 'col'), may hold values from 0.5 to 1.5
- norm1_shift: bfloat16 [2, 1024], P('section', 'col'), may hold values from -1.75 to 1.75
- qkv_weight: bfloat16 [2, 1024, 3, 1024], P('section', 'row', None, 'col'), may hold values from -0.1875 to 0.1875
- qv_bias: bfloat16 [2, 2, 1024], P('section', None, 'col'), may hold values from -3 to 3
- out_weight: bfloat16 [2, 1024, 1024], P('section', 'col', 'row'), may hold values from -1 to 1
- out_bias: bfloat16 [2, 1024], P('section', 'col'), may hold values from -1.75 to 1.75
- norm2_gain: bfloat16 [2, 1024], P('section', 'col'), may hold values from 0.5 to 1.5
- norm2_shift: bfloat16 [2, 1024], P('section', 'col'), may hold values from -1.75 to 1.75
- up_weight: bfloat16 [2, 1024, 4096], P('section', 'row', 'col'), may hold values from -1 to 1
- up_bias: bfloat16 [2, 4096], P('section', 'col'), may hold values from -3 to 3
- down_weight: bfloat16 [2, 4096, 1024], P('section', 'col', 'row'), may hold values from -0.09375 to 0.09375
- down_bias: bfloat16 [2, 1024], P('section', 'col'), may hold values from -1.75 to 1.75
Outputs:
- final_output: bfloat16 [2, 16, 577, 1024], P('section', 'row', None, 'col')
- input_grad: bfloat16 [2, 16, 577, 1024], P('section', 'row', None, 'col')
- norm1_gain_grad: float32 [2, 1024], P('section', 'col')
- norm1_shift_grad: float32 [2, 1024], P('section', 'col')
- qkv_weight_grad: float32 [2, 1024, 3, 1024], P('section', 'row', None, 'col')
- qv_bias_grad: float32 [2, 2, 1024], P('section', None, 'col')
- out_weight_grad: float32 [2, 1024, 1024], P('section', 'col', 'row')
- out_bias_grad: float32 [2, 1024], P('section', 'col')
- norm2_gain_grad: float32 [2, 1024], P('section', 'col')
- norm2_shift_grad: float32 [2, 1024], P('section', 'col')
- up_weight_grad: float32 [2, 1024, 4096], P('section', 'row', 'col')
- up_bias_grad: float32 [2, 4096], P('section', 'col')
- down_weight_grad: float32 [2, 4096, 1024], P('section', 'col', 'row')
- down_bias_grad: float32 [2, 1024], P('section', 'col')
The draws below stay inside these ranges and needn't reach their ends.
All inputs are finite; a program needn't handle non-finite values.
Results may differ from the reference program's by a relative error of at most 0.02.
Values may be sent and summed in bfloat16 or wider, within the bound.
No kernel may reach another device: no remote copies, remote signals or barrier semaphores. Data moves between devices by JAX's collectives and lax.ppermute only.
A program may use at most 192 MiB of HBM per device.

```python
import jax
import jax.numpy as jnp
from jax import lax

D = 1024
HEADS = 16
HD = 64
FF = 4096
SEQ = 577
IMAGES = 16
MB = 2
SECTIONS = 2


def draw_up_weight(key, part):
    key = jax.random.fold_in(key, 7)
    base_key, common_key = jax.random.split(key)
    base = jax.random.truncated_normal(base_key, -4.0, 4.0, (SECTIONS, D, FF), jnp.float32)
    common = 0.5 * jax.random.truncated_normal(common_key, -4.0, 4.0, (SECTIONS, 1, FF), jnp.float32)
    scale = 1.0 / D ** 0.5
    return ((base + common) * scale).astype(jnp.bfloat16)


def level_of(rng, extent, shards, smallest, top_value):
    def one(axis_at, shards_of):
        heights = jax.random.uniform(jax.random.fold_in(jax.random.fold_in(rng, 6), axis_at), (shards_of,), jnp.float32, smallest / len(shards), top_value / len(shards))
        return jnp.repeat(jnp.exp(heights), extent[axis_at] // shards_of).reshape((-1,) + (1,) * (len(extent) - axis_at - 1))

    level = one(*shards[0])
    for cut in shards[1:]:
        level = level * one(*cut)
    return level


def centred(own_key, dims, scale, limit, cuts=(), kind=jnp.bfloat16):
    drawn = scale * jax.random.normal(own_key, dims, jnp.float32)
    if cuts:
        drawn = drawn * level_of(own_key, dims, cuts, -0.22, 0.18)
    return jnp.clip(drawn, -limit, limit).astype(kind)


def setup_inputs(seed: int = 0) -> dict:
    arg_keys = jax.random.split(jax.random.key(seed), 15)
    layer_input = centred(arg_keys[0], (MB, IMAGES, SEQ, D), 1.0, 6.0, ((0, 2), (1, 16), (3, 4)))
    cotangent = centred(arg_keys[1], (MB, IMAGES, SEQ, D), 1.0, 6.0, ((0, 2), (1, 16), (3, 4)))
    norm1_gain = jnp.clip(1.0 + 0.1 * jax.random.normal(arg_keys[2], (SECTIONS, D), jnp.float32), 0.5, 1.5).astype(jnp.bfloat16)
    norm1_shift = centred(arg_keys[3], (SECTIONS, D), 0.3, 1.75, ((0, 2), (1, 4)))
    qkv_weight = centred(arg_keys[4], (SECTIONS, D, 3, D), D ** -0.5, 0.1875, ((0, 2), (1, 16), (3, 4)))
    qv_bias = centred(arg_keys[5], (SECTIONS, 2, D), 0.5, 3.0, ((0, 2), (2, 4)))
    out_weight = centred(arg_keys[6], (SECTIONS, D, D), (max(D // 32, 8)) ** -0.5, 1.0, ((0, 2), (1, 4), (2, 16)))
    out_bias = centred(arg_keys[7], (SECTIONS, D), 0.3, 1.75, ((0, 2), (1, 4)))
    norm2_gain = jnp.clip(1.0 + 0.1 * jax.random.normal(arg_keys[8], (SECTIONS, D), jnp.float32), 0.5, 1.5).astype(jnp.bfloat16)
    norm2_shift = centred(arg_keys[9], (SECTIONS, D), 0.3, 1.75, ((0, 2), (1, 4)))
    up_weight = draw_up_weight(jax.random.fold_in(arg_keys[14], 71), 0)
    up_bias = centred(arg_keys[11], (SECTIONS, FF), 0.5, 3.0, ((0, 2), (1, 4)))
    down_weight = centred(arg_keys[12], (SECTIONS, FF, D), FF ** -0.5, 0.09375, ((0, 2), (1, 4), (2, 16)))
    down_bias = centred(arg_keys[13], (SECTIONS, D), 0.3, 1.75, ((0, 2), (1, 4)))
    return dict(layer_input=layer_input, cotangent=cotangent, norm1_gain=norm1_gain, norm1_shift=norm1_shift, qkv_weight=qkv_weight, qv_bias=qv_bias, out_weight=out_weight, out_bias=out_bias, norm2_gain=norm2_gain, norm2_shift=norm2_shift, up_weight=up_weight, up_bias=up_bias, down_weight=down_weight, down_bias=down_bias)


EPS = 1e-06
HIGHEST_PRECISION = lax.Precision.HIGHEST

@jax.custom_vjp
def low(v):
    return lax.optimization_barrier(v.astype(jnp.bfloat16)).astype(jnp.float32)

@jax.custom_vjp
def low_back(v):
    return v

def low_keep(v):
    return (low(v), None)

def low_pass(kept, grad):
    return (grad,)

def back_keep(v):
    return (v, None)

def back_low(kept, grad):
    return (low(grad),)
low.defvjp(low_keep, low_pass)
low_back.defvjp(back_keep, back_low)

def rounded(value):
    return low(low_back(value))

def matmul(form, left, right):
    return jnp.einsum(form, left, right, precision=HIGHEST_PRECISION)

def layer_norm(resid, gain, shift):
    center = lax.optimization_barrier(jnp.mean(resid, -1, keepdims=True))
    spread = lax.optimization_barrier(jnp.mean(resid * resid, -1, keepdims=True)) - center * center
    return (resid - center) * lax.rsqrt(spread + EPS) * gain + shift

def attend(block):
    queries, keys, values = block
    scores = low_back(matmul('qhd,khd->hqk', queries, keys) * 0.125)
    probs = jax.nn.softmax(scores, axis=-1)
    return matmul('hqk,khd->qhd', low(probs), values)

def layer(resid, weights):
    norm1_gain, norm1_shift, qkv_weight, qv_bias, out_weight, out_bias, norm2_gain, norm2_shift, up_weight, up_bias, down_weight, down_bias = weights
    images, length, width = resid.shape
    normed = low(layer_norm(resid, norm1_gain, norm1_shift))
    mixed = matmul('isd,dtc->istc', normed, qkv_weight)
    queries = rounded(mixed[:, :, 0] + qv_bias[0]).reshape(images, length, HEADS, HD)
    keys = rounded(mixed[:, :, 1]).reshape(images, length, HEADS, HD)
    values = rounded(mixed[:, :, 2] + qv_bias[1]).reshape(images, length, HEADS, HD)
    context = lax.map(jax.checkpoint(attend), (queries, keys, values))
    context = rounded(context.reshape(images, length, width))
    attention = low_back(matmul('isc,cd->isd', context, out_weight) + out_bias)
    middle = resid + attention
    normed_two = low(layer_norm(middle, norm2_gain, norm2_shift))
    hidden = low_back(matmul('isd,df->isf', normed_two, up_weight) + up_bias)
    active = low(jax.nn.gelu(hidden, approximate=False))
    return middle + low_back(matmul('isf,fd->isd', active, down_weight) + down_bias)

def reference(layer_input, cotangent, norm1_gain, norm1_shift, qkv_weight, qv_bias, out_weight, out_bias, norm2_gain, norm2_shift, up_weight, up_bias, down_weight, down_bias):
    params = tuple((weight_arg.astype(jnp.float32) for weight_arg in (norm1_gain, norm1_shift, qkv_weight, qv_bias, out_weight, out_bias, norm2_gain, norm2_shift, up_weight, up_bias, down_weight, down_bias)))

    def run(inputs, stacked):
        first_weights = tuple((entry[0] for entry in stacked))
        second_weights = tuple((entry[1] for entry in stacked))
        outputs = []
        for micro in range(MB):
            middle_section = rounded(layer(inputs[micro], first_weights))
            outputs.append(layer(middle_section, second_weights))
        return jnp.stack(outputs)
    final, pullback = jax.vjp(run, layer_input.astype(jnp.float32), params)
    input_grad, grads = pullback(cotangent.astype(jnp.float32))
    return (final.astype(jnp.bfloat16), input_grad.astype(jnp.bfloat16), grads[0], grads[1], grads[2], grads[3], grads[4], grads[5], grads[6], grads[7], grads[8], grads[9], grads[10], grads[11])
```

```python
import functools

import jax
import jax.numpy as jnp
from jax import lax
from jax.experimental import pallas as pl
from jax.experimental.pallas import tpu as pltpu
from jax.sharding import PartitionSpec as P

HD = 64
EPS = 1e-06
TOKENS = 577
HALF = 304
ROWS = 2 * HALF
D = 1024
BF16 = jnp.bfloat16
F32 = jnp.float32
VMEM_LIMIT = 24 * 1024 * 1024


def swap(value, axis, mask):
    return lax.ppermute(value, axis, [(i, i ^ mask) for i in range(lax.axis_size(axis))])


def after(value, *marks):
    return lax.optimization_barrier((value,) + marks)[0]


def dot(left, right, left_dim, right_dim):
    return lax.dot_general(
        left, right, (((left_dim,), (right_dim,)), ((), ())), preferred_element_type=F32
    )


class Place:
    def __init__(self):
        self.section = lax.axis_index("section")
        col = lax.axis_index("col")
        self.y = col // 2
        self.core = col % 2
        self.col = col


UNIT = {"x": 4, "z": 1}
MASKS = (3, 1)
LIGHT = {"x": "z", "z": "x"}


def ring_blocks(name):
    row = lax.axis_index("row")
    here = row // 4 if name == "x" else row % 4
    first, second = MASKS
    return here, here ^ first, here ^ second, here ^ first ^ second


def call(kernel, outs, ins, name, scratch=()):
    return pl.pallas_call(
        kernel,
        out_shape=[jax.ShapeDtypeStruct(*out) for out in outs],
        scratch_shapes=list(scratch),
        compiler_params=pltpu.CompilerParams(vmem_limit_bytes=VMEM_LIMIT),
        cost_estimate=pl.CostEstimate(flops=0, bytes_accessed=0, transcendentals=0),
        name=name,
    )(*ins)


def place_kernel(name, dim, *refs):
    *pieces, out = refs
    for piece, block in zip(pieces, ring_blocks(name)):
        if dim == 0:
            out[block] = piece[...]
        else:
            out[:, block] = piece[...]


def place_halves_kernel(name, dim, own, near, far, low, high, out):
    blocks = ring_blocks(name)
    half = low.shape[0]
    for piece, block in zip((own, near, far), blocks):
        if dim == 0:
            out[block] = piece[...]
        else:
            out[:, block] = piece[...]
    if dim == 0:
        out[blocks[3], :half] = low[...]
        out[blocks[3], half:] = high[...]
    else:
        out[:half, blocks[3]] = low[...]
        out[half:, blocks[3]] = high[...]


def ring_gather(value, name, dim, *middle):
    first, second = (mask * UNIT[name] for mask in MASKS)
    near = swap(value, "row", first)
    far = swap(value, "row", second)
    both = swap(after(near, *middle) if middle else near, "row", second)
    shape = value.shape[:dim] + (4,) + value.shape[dim:]
    kernel = functools.partial(place_kernel, name, dim)
    return call(kernel, [(shape, BF16)], (value, near, far, both), "place_blocks")[0]


def gather_light(shard, stream, *middle):
    part = ring_gather(shard, LIGHT[stream], 0, *middle)
    return part.reshape(256, shard.shape[1]) if stream == "x" else part


class Heavy:
    def __init__(self, part, stream):
        self.part, self.stream = part, stream
        self.first, self.second = (mask * UNIT[stream] for mask in MASKS)
        self.near = swap(part, "row", self.first)
        self.far = swap(part, "row", self.second)

    def finish(self, *marks):
        near, far = lax.optimization_barrier((self.near, self.far) + marks)[:2]
        half = near.shape[0] // 2
        self.sent = (near[:half], far[half:])
        self.low = low = swap(self.sent[0], "row", self.second)
        self.high = high = swap(self.sent[1], "row", self.first)
        dim = 0 if self.stream == "x" else 1
        shape = near.shape[:dim] + (4,) + near.shape[dim:]
        kernel = functools.partial(place_halves_kernel, self.stream, dim)
        ins = (self.part, near, far, low, high)
        return call(kernel, [(shape, BF16)], ins, "place_blocks")[0].reshape(D, -1)


def pack_kernel(*refs):
    *ins, out = refs
    for index, value in enumerate(ins[:6]):
        out[index : index + 1] = value[...]
    out[6:8] = ins[6][0]
    for index in range(4):
        out[8 + index : 9 + index] = ins[7][:, 256 * index : 256 * index + 256]
    out[12:16] = jnp.zeros((4, 256), BF16)


def join(refs, out):
    start = 0
    for ref in refs:
        out[start : start + ref.shape[0]] = ref[...]
        start += ref.shape[0]


def grads_kernel(x_widths, z_widths, done, ride, *refs):
    refs = list(refs)
    tile, left = refs.pop(), refs.pop()
    first = 3 * len(x_widths + z_widths)
    extra = refs[first : first + 10]
    if ride:
        rows = refs[first + 10 * done][...].astype(BF16)
        for out in refs[-10:][3:5]:
            out[128:144] = rows[:, :512]
            out[144:160] = rows[:, 512:]

    def blocks(stream, width, store):
        one, other, right = (refs.pop(0) for _ in range(3))
        join((one, other), left)
        for low in range(0, width, 256):
            columns = slice(low, low + 256)
            if stream == "x":
                for index, block in enumerate(ring_blocks("x")):
                    at = pl.ds(pl.multiple_of(block * 256, 256), 256)
                    store(index, None, low, dot(left[:, at], right[:, columns], 0, 0))
                continue
            for x in range(4):
                tile[...] = dot(left[:, 256 * x : 256 * x + 256], right[:, columns], 0, 0)
                for index, block in enumerate(ring_blocks("z")):
                    rows = pl.ds(pl.multiple_of(block * 64, 64), 64)
                    store(index, x, low, tile[rows, :])

    outs = refs[-10:]
    for stream, widths, out in (("x", x_widths, outs[:5]), ("z", z_widths, outs[5:])):
        start = 0
        for width in widths:

            def store(index, x, low, value):
                columns = slice(start + low, start + low + 256)
                value = value.astype(BF16)
                if index < 3:
                    if x is None:
                        out[index][:, columns] = value
                    else:
                        out[index][x, :, columns] = value
                elif x is None:
                    out[3][:128, columns] = value[:128]
                    out[4][:128, columns] = value[128:]
                else:
                    out[3 + x // 2][x % 2, :, columns] = value

            blocks(stream, width, store)
            start += width
        for index in range(5 if done else 0):
            out[index][..., start:] = extra[(0 if stream == "x" else 5) + index][...]


def weight_grads(x_parts, z_parts, name, done=(), ride=()):
    ins, widths = [], ([], [])
    extra = done[0].shape[-1] if done else 0
    for index, parts in enumerate((x_parts, z_parts)):
        for halves, right in parts:
            ins += [*halves, right]
            widths[index].append(right.shape[1])
    outs = []
    for lead, total in (((256,), sum(widths[0]) + extra), ((4, 64), sum(widths[1]) + extra)):
        half = (lead[0] // 2,) + lead[1:]
        if ride and len(lead) == 1:
            half = (half[0] + 32,)
        outs += [lead + (total,)] * 3 + [half + (total,)] * 2
    outs = call(
        functools.partial(grads_kernel, tuple(widths[0]), tuple(widths[1]), bool(done), bool(ride)),
        [(out, BF16) for out in outs],
        ins + list(done) + list(ride),
        name,
        scratch=(pltpu.VMEM((ROWS, D), BF16), pltpu.VMEM((256, 256), F32)),
    )
    return tuple(outs)


def rider(rows):
    if rows.shape[0] == 32:
        return jnp.concatenate([rows[:16], rows[16:]], 1)
    return rows[:, :D]


def join_kernel(ride, *refs):
    refs = list(refs)
    part_out = refs.pop() if ride else None
    own_out, near_out, far_out = refs[-3:]
    ins = refs[: -4 if ride else -3]
    start = 0
    for index in range(0, len(ins), 5):
        own, near, far, low, high = ins[index : index + 5]
        size = near.shape[0]
        half = size // 2
        columns = slice(start, start + own.shape[-1])
        own_out[..., columns] = own[...]
        near_out[:half, ..., columns] = (
            near[:half].astype(F32) + low[:half].astype(F32)
        ).astype(BF16)
        near_out[half:size, ..., columns] = near[half:]
        far_out[:half, ..., columns] = far[:half]
        far_out[half:, ..., columns] = (far[half:].astype(F32) + high[:half].astype(F32)).astype(BF16)
        if low.shape[0] > half:
            passed = rider(low[half:])
            near_out[size:, :D] = passed
            near_out[size:, D:] = jnp.zeros((16, near_out.shape[1] - D), BF16)
            part_out[...] = (
                refs[-4][...] + passed.astype(F32) + rider(high[half:]).astype(F32)
            )
        start += own.shape[-1]


def split_kernel(stream, groups, ride, *refs):
    refs = list(refs)
    total = refs.pop()
    sums_out = refs.pop() if ride else None
    own, near, far, low, high = refs[-5:]
    ins = refs[:-5]
    if ride:
        sums = ins.pop()[...] + rider(ins[1][256:]).astype(F32)
        sums_out[...] = sums
        for out in (low, high):
            out[32:, :D] = sums.astype(BF16)
            out[32:, D:] = jnp.zeros((16, out.shape[1] - D), BF16)
    blocks = ring_blocks(LIGHT[stream])
    start = 0
    for count in groups:
        parts, ins = ins[:count], ins[count:]
        width = parts[0].shape[-1]
        value = parts[0][...].astype(F32)
        for part in parts[1:]:
            value += part[: value.shape[0]].astype(F32)
        total[..., :width] = value
        columns = slice(start, start + width)
        for out, block in zip((own, near, far, None), blocks):
            if stream == "x":
                rows = pl.ds(pl.multiple_of(block * 64, 64), 64)
                value = total[rows, :width].astype(BF16)
            else:
                value = total[block, :, :width].astype(BF16)
            if out is None:
                low[:32, columns] = value[:32]
                high[:32, columns] = value[32:]
            else:
                out[:, columns] = value
        start += width


def split(stream, groups, ride):
    width = sum(group[0].shape[-1] for group in groups)
    widest = max(group[0].shape[-1] for group in groups)
    half = 48 if ride else 32
    return call(
        functools.partial(split_kernel, stream, tuple(len(group) for group in groups), bool(ride)),
        [((rows, width), BF16) for rows in (64, 64, 64, half, half)] + [((16, D), F32)] * len(ride),
        [part for group in groups for part in group] + list(ride),
        "split_blocks",
        scratch=(pltpu.VMEM(groups[0][0].shape[:-1] + (widest,), F32),),
    )


def over_far(name, value):
    return swap(value, "row", MASKS[1] * UNIT[name])


def over_near(name, value):
    return swap(value, "row", MASKS[0] * UNIT[name])


class Ring:
    def __init__(self, name, own, near, far, low, high):
        self.name, self.own, self.near, self.far = name, own, near, far
        self.low, self.high = over_far(name, low), over_near(name, high)

    def finish(self, *marks, beside=(), ride=()):
        rings = (self,) + tuple(beside)
        ins = [part for ring in rings for part in (ring.own, ring.near, ring.far)]
        ins = lax.optimization_barrier((*ins, *marks))[: len(ins)]
        shape = self.own.shape[:-1] + (sum(ring.own.shape[-1] for ring in rings),)
        wide = (shape[0] + 16 * len(ride),) + shape[1:]
        ins = [
            part
            for index, ring in enumerate(rings)
            for part in (*ins[3 * index : 3 * index + 3], ring.low, ring.high)
        ]
        outs = [(shape, BF16), (wide, BF16), (shape, BF16)] + [((16, D), F32)] * len(ride)
        kernel = functools.partial(join_kernel, bool(ride))
        own, near, far, *self.ride = call(kernel, outs, ins + list(ride), "join_blocks")
        self.sent = near, far
        return own, over_near(self.name, near), over_far(self.name, far)


def light_ring(stream, *groups, ride=()):
    own, near, far, low, high, *ride = split(stream, groups, ride)
    ring = Ring(LIGHT[stream], own, near, far, low, high)
    ring.riding = ride
    return ring


def light_sum(ring, *marks):
    own, near, far = ring.finish(*marks, ride=ring.riding)
    total = own.astype(F32) + near[:64].astype(F32) + far.astype(F32)
    if not ring.riding:
        return total
    return total, ring.ride[0] + near[64:, :D].astype(F32)


def column_sums(own, other):
    return jnp.sum(own[...].astype(F32), 0, keepdims=True) + jnp.sum(
        other[...].astype(F32), 0, keepdims=True
    )


def head_mask(head):
    lane = lax.broadcasted_iota(jnp.int32, (1, 256), 1)
    return lane // HD == head


QUERY_CUTS = ((0, HALF), (HALF, ROWS))
GRAD_CUTS = ((0, 256), (256, 512), (512, ROWS))
HALVES = (slice(0, HALF), slice(HALF, ROWS))


def attend_forward_kernel(
    own, other, weights, bias, qv_bias, q_out, k_out, v_out, context, send, mine
):
    for rows, part in zip(HALVES, (own, other)):
        mixed = dot(part[...], weights[:, :768], 1, 0)
        q_out[rows] = (mixed[:, :256] + qv_bias[:, :256]).astype(BF16)
        k_out[rows] = mixed[:, 256:512].astype(BF16)
        v_out[rows] = (mixed[:, 512:] + qv_bias[:, 256:]).astype(BF16)
    for low, high in QUERY_CUTS:
        total = jnp.zeros((high - low, 256), F32)
        for head in range(4):
            mask = head_mask(head)
            queries = jnp.where(mask, q_out[low:high].astype(F32) * 0.125, 0.0).astype(BF16)
            scores = dot(queries, k_out[...], 1, 1) + bias[...]
            raised = jnp.exp(scores - jnp.max(scores, -1, keepdims=True))
            share = 1.0 / jnp.sum(raised, -1, keepdims=True)
            total = jnp.where(mask, dot(raised.astype(BF16), v_out[...], 1, 0) * share, total)
        context[low:high] = total.astype(BF16)
    send[...] = dot(context[HALVES[1]], weights[:, 768:], 1, 1).astype(BF16)
    mine[...] = dot(context[HALVES[0]], weights[:, 768:], 1, 1)


def attend_forward(own, other, weights, bias, qv_bias):
    wide, half = (ROWS, 256), (HALF, D)
    return call(
        attend_forward_kernel,
        [(wide, BF16)] * 4 + [(half, BF16), (half, F32)],
        (own, other, weights, bias, qv_bias),
        "attend_forward",
    )


def attend_backward_kernel(
    own, other, weights, bias, q_in, k_in, v_in, grad_qk, grad_v, sums, ends, send, mine, keep, turned, tall
):
    for rows, part in zip(HALVES, (own, other)):
        keep[rows] = dot(part[...], weights[:, 768:], 1, 0).astype(BF16)
    turned[...] = jnp.zeros_like(turned)
    tall[ROWS:] = jnp.zeros((640 - ROWS, 256), F32)
    for head in range(4):
        mask = head_mask(head)
        tall[:ROWS] = jnp.where(mask, k_in[...].astype(F32) * 0.125, 0.0)
        keys = tall[:ROWS].astype(BF16)
        flat_keys = tall[...].T[:, :ROWS].astype(BF16)
        values = jnp.where(mask, v_in[...], 0.0).astype(BF16)
        total_k = jnp.zeros((ROWS, 256), F32)
        total_v = jnp.zeros((ROWS, 256), F32)
        for low, high in GRAD_CUTS:
            queries = q_in[low:high]
            scores = dot(keys, queries, 1, 1) + bias[...]
            raised = jnp.exp(scores - jnp.max(scores, 0, keepdims=True))
            probs = raised * (1.0 / jnp.sum(raised, 0, keepdims=True))
            grads = dot(values, keep[low:high], 1, 1)
            inner = jnp.sum(probs * grads, 0, keepdims=True)
            grad_scores = (probs * (grads - inner)).astype(BF16)
            total_k += dot(grad_scores, queries, 1, 0)
            total_v += dot(probs.astype(BF16), keep[low:high], 1, 0)
            turned[:, low:high] += dot(flat_keys, grad_scores, 1, 0)
        columns = slice(256, 512)
        if head:
            total_k = jnp.where(mask, total_k * 0.125, grad_qk[:, columns].astype(F32))
            total_v = jnp.where(mask, total_v, grad_v[...].astype(F32))
        else:
            total_k = total_k * 0.125
        grad_qk[:, columns] = total_k.astype(BF16)
        grad_v[...] = total_v.astype(BF16)
    grad_qk[:, :256] = turned[...].T[:ROWS].astype(BF16)
    sums[:, :256] = jnp.sum(grad_qk[:, :256].astype(F32), 0, keepdims=True)
    sums[:, 256:] = jnp.sum(grad_v[...].astype(F32), 0, keepdims=True)
    ends[...] = column_sums(own, other)
    for rows, out in zip(HALVES, (mine, send)):
        value = dot(grad_qk[rows], weights[:, :512], 1, 1)
        value += dot(grad_v[rows], weights[:, 512:768], 1, 1)
        out[...] = value.astype(out.dtype)


def attend_backward(own, other, weights, bias, queries, keys, values):
    half = (HALF, D)
    return call(
        attend_backward_kernel,
        [((ROWS, 512), BF16), ((ROWS, 256), BF16), ((1, 512), F32), ((1, D), F32)]
        + [(half, BF16), (half, F32)],
        (own, other, weights, bias, queries, keys, values),
        "attend_backward",
        scratch=(
            pltpu.VMEM((ROWS, 256), BF16),
            pltpu.VMEM((256, 640), F32),
            pltpu.VMEM((640, 256), F32),
        ),
    )


def mlp_forward_kernel(own, other, up, down, up_bias, active, slope, send, mine):
    for rows, part in zip(HALVES, (own, other)):
        for low in range(0, D, 256):
            columns = slice(low, low + 256)
            hidden = dot(part[...], up[:, columns], 1, 0) + up_bias[:, columns]
            share = 0.5 * (1.0 + lax.erf(hidden * 0.7071067811865476))
            density = 0.3989422804014327 * jnp.exp(-0.5 * hidden * hidden)
            active[rows, columns] = (hidden * share).astype(BF16)
            slope[rows, columns] = (share + hidden * density).astype(BF16)
    send[...] = dot(active[HALVES[1]], down[...], 1, 1).astype(BF16)
    mine[...] = dot(active[HALVES[0]], down[...], 1, 1)


def mlp_forward(own, other, up, down, up_bias):
    whole, half = (ROWS, D), (HALF, D)
    return call(
        mlp_forward_kernel,
        [(whole, BF16), (whole, BF16), (half, BF16), (half, F32)],
        (own, other, up, down, up_bias),
        "mlp_forward",
    )


def mlp_backward_kernel(own, other, up, down, slope, grad_hidden, sums, ends, send, mine):
    for rows, part in zip(HALVES, (own, other)):
        for low in range(0, D, 256):
            columns = slice(low, low + 256)
            value = dot(part[...], down[:, columns], 1, 0) * slope[rows, columns].astype(F32)
            grad_hidden[rows, columns] = value.astype(BF16)
    send[...] = dot(grad_hidden[HALVES[1]], up[...], 1, 1).astype(BF16)
    mine[...] = dot(grad_hidden[HALVES[0]], up[...], 1, 1)
    sums[...] = jnp.sum(grad_hidden[...].astype(F32), 0, keepdims=True)
    ends[...] = column_sums(own, other)


def mlp_backward(own, other, up, down, slope):
    whole, half = (ROWS, D), (HALF, D)
    return call(
        mlp_backward_kernel,
        [(whole, BF16), ((1, D), F32), ((1, D), F32), (half, BF16), (half, F32)],
        (own, other, up, down, slope),
        "mlp_backward",
    )


def feature_pairs(value, other, place):
    low = jnp.where(place.y == 0, value, other)
    high = jnp.where(place.y == 0, other, value)
    pair = jnp.concatenate([low, high], 1)
    return pair, swap(pair, "col", 1)


def gather_features(value, other, place):
    pair, arrived = feature_pairs(value, other, place)
    even = jnp.where(place.core == 0, pair, arrived)
    odd = jnp.where(place.core == 0, arrived, pair)
    return jnp.concatenate([even[:, :256], odd[:, :256], even[:, 256:], odd[:, 256:]], 1)


def whole_rows(pair, arrived, rows):
    core = lax.rem(lax.axis_index("col"), 2) == 0
    mine, other = pair[rows], arrived[rows]
    even, odd = jnp.where(core, mine, other), jnp.where(core, other, mine)
    return jnp.concatenate([even[:, :256], odd[:, :256], even[:, 256:], odd[:, 256:]], 1)


def halves_of(pair, arrived):
    core = lax.rem(lax.axis_index("col"), 2) == 0
    first = whole_rows(pair, arrived, slice(0, HALF))
    second = whole_rows(pair, arrived, slice(HALF, TOKENS))
    second = jnp.concatenate([second, jnp.zeros((ROWS - TOKENS, D), BF16)], 0)
    return jnp.where(core, first, second), jnp.where(core, second, first)


def order_kernel(pair, arrived, own, other):
    own[...], other[...] = halves_of(pair, arrived)


def order_halves(pair, arrived):
    return call(order_kernel, [((HALF, D), BF16)] * 2, (pair, arrived), "order_halves")


def enter_kernel(pair, arrived, gain, shift, resid, own, other):
    for out, value in zip((own, other), halves_of(pair, arrived)):
        value = value.astype(F32)
        if out is own:
            resid[...] = value
        out[...] = (norm(value)[0] * gain[...] + shift[...]).astype(BF16)


def enter(pair, arrived, gain, shift):
    half = (HALF, D)
    outs = [(half, F32), (half, BF16), (half, BF16)]
    return call(enter_kernel, outs, (pair, arrived, gain, shift), "enter")


def pick_kernel(own, kept, sent):
    col = lax.axis_index("col")
    for out, block in ((kept, col), (sent, col ^ 1)):
        out[...] = own[:, pl.ds(pl.multiple_of(block * 256, 256), 256)]


def merge_kernel(kept, arrived, out):
    core = lax.rem(lax.axis_index("col"), 2) == 0
    mine, other = kept[...], arrived[...]
    out[:HALF] = jnp.where(core, mine, other)
    out[HALF:] = jnp.where(core, other, mine)[: TOKENS - HALF]


def feature_block(own):
    part = ((HALF, 256), BF16)
    kept, sent = call(pick_kernel, [part, part], (own,), "pick_block")
    return call(
        merge_kernel, [((TOKENS, 256), BF16)], (kept, swap(sent, "col", 1)), "merge_block"
    )[0]


def small_kernel(sums, halves, arrived, *outs):
    col = lax.axis_index("col")
    columns = pl.ds(pl.multiple_of(col * 256, 256), 256)
    for index in range(6):
        value = (halves if index < 4 else sums)[index : index + 1, columns]
        if index < 2:
            value += arrived[index : index + 1, columns]
        outs[index][...] = value
    for index in range(2):
        outs[6][:, index] = sums[6:7, 256 * index : 256 * index + 256]
    outs[7][...] = sums[7:8]


def chip_sum(send, mine):
    return (mine + swap(send, "col", 1).astype(F32)).astype(BF16)


def col_sum(chip, arrived):
    return chip.astype(F32) + arrived.astype(F32)


def norm(resid):
    center = jnp.mean(resid, -1, keepdims=True)
    scale = lax.rsqrt(jnp.mean(resid * resid, -1, keepdims=True) - center * center + EPS)
    return (resid - center) * scale, scale


def norm_backward_kernel(chip, arrived, resid, gain, grad_out, *outs):
    grad = chip[...].astype(F32) + arrived[...].astype(F32)
    normal, scale = norm(resid[...])
    scaled = grad * gain[...]
    mean_one = jnp.mean(scaled, -1, keepdims=True)
    mean_two = jnp.mean(scaled * normal, -1, keepdims=True)
    total = grad_out[...].astype(F32) + scale * (scaled - mean_one - normal * mean_two)
    outs[0][...] = total.astype(BF16)
    if len(outs) > 1:
        outs[1][0:1] = jnp.sum(grad * normal, 0, keepdims=True)
        outs[1][1:2] = jnp.sum(grad, 0, keepdims=True)
        outs[2][...] = total


def norm_backward(chip, arrived, resid, gain, grad_out, wide):
    half = (HALF, D)
    outs = [(half, BF16)] + [((2, D), F32), (half, F32)] * wide
    return call(norm_backward_kernel, outs, (chip, arrived, resid, gain, grad_out), "norm_backward")


def norm_sums_kernel(chip, resid, sums):
    grad = chip[...].astype(F32)
    sums[0:1] = jnp.sum(grad * norm(resid[...])[0], 0, keepdims=True)
    sums[1:2] = jnp.sum(grad, 0, keepdims=True)


def norm_sums(chip, resid):
    return call(norm_sums_kernel, [((2, D), F32)], (chip, resid), "norm_sums")[0]


def pack_sums_kernel(*refs):
    *ins, out = refs
    for layer in range(2):
        one, two, qv, hidden, attend, mlp = ins[6 * layer : 6 * layer + 6]
        row = 8 * layer
        out[row : row + 2] = one[...]
        out[row + 2 : row + 4] = two[...]
        out[row + 4 : row + 5] = attend[...]
        out[row + 5 : row + 6] = mlp[...]
        out[row + 6 : row + 7, :512] = qv[...]
        out[row + 6 : row + 7, 512:] = jnp.zeros((1, 512), F32)
        out[row + 7 : row + 8] = hidden[...]


def mlp_part(ends, saved, weights):
    _, up, down = weights
    resid, one, qkv, context, middle, two, active, slope = saved
    grad_hidden, hidden_sum, mlp_sum, send, mine = mlp_backward(*ends, up, down, slope)
    chip = chip_sum(send, mine)
    pinned = lax.optimization_barrier((*two, *ends, grad_hidden, active, chip))
    two, ends, (grad_hidden, active) = pinned[0:2], pinned[2:4], pinned[4:6]
    return chip, swap(chip, "col", 2), (two, ends, grad_hidden, active), hidden_sum, mlp_sum


def attend_part(pair, saved, weights, bias, marks=()):
    resid, one, qkv, context, middle, two, active, slope = saved
    tall_bias = bias.reshape(ROWS, 1)
    grad_qk, grad_v, qv_sum, attend_sum, send, mine = attend_backward(
        *pair, weights[0], tall_bias, *qkv
    )
    chip = chip_sum(after(send, *marks) if marks else send, mine)
    pinned = lax.optimization_barrier((*one, *pair, grad_qk, grad_v, context, chip))
    one, pair, (grad_qk, grad_v, context) = pinned[0:2], pinned[2:4], pinned[4:7]
    parts = [(one, grad_qk)], [(one, grad_v), (pair, context)]
    return chip, swap(chip, "col", 2), parts, qv_sum, attend_sum


def local(
    layer_input,
    cotangent,
    norm1_gain,
    norm1_shift,
    qkv_weight,
    qv_bias,
    out_weight,
    out_bias,
    norm2_gain,
    norm2_shift,
    up_weight,
    up_bias,
    down_weight,
    down_bias,
):
    place = Place()
    leading = place.section == 0

    vectors = call(
        pack_kernel,
        [((16, 256), BF16)],
        (norm1_gain, norm1_shift, norm2_gain, norm2_shift, out_bias, down_bias, qv_bias, up_bias),
        "pack_vectors",
    )[0]
    narrow = [qkv_weight[0, :, 0], qkv_weight[0, :, 1], qkv_weight[0, :, 2], out_weight[0].T]
    attend_mine = jnp.concatenate(narrow, 1)
    mlp_mine = jnp.concatenate([up_weight[0], down_weight[0].T], 1)
    attend_other = swap(attend_mine, "section", 1)
    entry = layer_input[0, 0]
    entry_other = swap(entry, "col", 2)
    vectors_other = swap(vectors, "section", 1)
    mlp_other = swap(after(mlp_mine, attend_mine), "section", 1)
    attend = (
        jnp.where(leading, attend_mine, attend_other),
        jnp.where(leading, attend_other, attend_mine),
    )
    attend0 = gather_light(attend[0], "x")
    entry, entry_other, vectors, vectors_other, mlp_mine, mlp_other, _ = lax.optimization_barrier(
        (entry, entry_other, vectors, vectors_other, mlp_mine, mlp_other, attend0)
    )
    attend0 = Heavy(attend0, "x")
    marks = (attend0.near, attend0.far)
    attend0 = attend0.finish()

    vectors = (
        jnp.where(leading, vectors, vectors_other),
        jnp.where(leading, vectors_other, vectors),
    )
    both = jnp.concatenate(vectors, 0)
    both = gather_features(both, swap(both, "col", 2), place).astype(F32)
    params = []
    for layer in range(2):
        wide = tuple(both[16 * layer + i][None] for i in range(6))
        narrow = vectors[layer].astype(F32)
        params.append(wide + (narrow[6:8].reshape(1, 512), narrow[8:12].reshape(1, 1024)))
    entry = feature_pairs(entry, entry_other, place)

    mlp = (
        jnp.where(leading, mlp_mine, mlp_other),
        jnp.where(leading, mlp_other, mlp_mine),
    )
    up0 = gather_light(mlp[0][:, :1024], "x", *marks)
    down0 = gather_light(mlp[0][:, 1024:], "z", *marks)
    exit_grad = after(cotangent[0, 0], *marks)
    exit_other = swap(exit_grad, "col", 2)

    position = lax.broadcasted_iota(jnp.int32, (1, ROWS), 1)
    valid = TOKENS - HALF
    padding = jnp.where(
        place.core == 0, position >= TOKENS, jnp.logical_and(position >= valid, position < HALF)
    )
    bias = jnp.where(padding, -1e30, 0.0).astype(F32)

    gain1, shift1, gain2, shift2, out_bias0, down_bias0, qv_bias0, up_bias0 = params[0]
    resid0, *one0 = enter(*entry, gain1, shift1)
    one0 = lax.optimization_barrier((*one0, up0, down0, exit_other))[:2]
    up_steps = Heavy(after(up0, attend0), "x")
    down_steps = Heavy(down0, "z")
    *qkv0, context0, send, mine = attend_forward(*one0, attend0, bias, qv_bias0)
    send = after(send, up_steps.near, up_steps.far, down_steps.near, down_steps.far)
    chip = chip_sum(send, mine)
    up0 = up_steps.finish(chip)
    down0 = down_steps.finish(chip)
    attend1 = gather_light(after(attend[1], chip), "x")
    attend_steps = Heavy(after(attend1, up_steps.low, up_steps.high), "x")
    arrived = after(swap(chip, "col", 2), up0, down0, attend1)
    middle0 = resid0 + col_sum(chip, arrived) + out_bias0
    normal, _ = norm(middle0)
    two_own = (normal * gain2 + shift2).astype(BF16)
    two0 = (two_own, swap(two_own, "col", 1))
    active0, slope0, send, mine = mlp_forward(*two0, up0, down0, up_bias0)
    chip = chip_sum(after(send, attend_steps.near, attend_steps.far), mine)
    attend1 = attend_steps.finish(chip)
    marks = (attend_steps.low, attend_steps.high)
    up1 = gather_light(after(mlp[1][:, :1024], send), "x", *marks)
    down1 = gather_light(after(mlp[1][:, 1024:], send), "z", *marks)
    arrived = after(swap(chip, "col", 2), attend1, up1, down1)
    section_mid = (middle0 + col_sum(chip, arrived) + down_bias0).astype(BF16)

    gain1, shift1, gain2, shift2, out_bias1, down_bias1, qv_bias1, up_bias1 = params[1]
    resid1 = section_mid.astype(F32)
    normal, _ = norm(resid1)
    one_own = (normal * gain1 + shift1).astype(BF16)
    one_own = after(one_own, up1, down1)
    one1 = (one_own, swap(one_own, "col", 1))
    up_steps = Heavy(after(up1, attend1), "x")
    down_steps = Heavy(down1, "z")
    *qkv1, context1, send, mine = attend_forward(*one1, attend1, bias, qv_bias1)
    send = after(send, up_steps.near, up_steps.far, down_steps.near, down_steps.far)
    chip = chip_sum(send, mine)
    up1 = up_steps.finish(chip)
    down1 = down_steps.finish(chip)
    ends = order_halves(*feature_pairs(exit_grad, exit_other, place))
    arrived = after(swap(chip, "col", 2), *ends, up1, down1)
    middle1 = resid1 + col_sum(chip, arrived) + out_bias1
    normal, _ = norm(middle1)
    two_own = (normal * gain2 + shift2).astype(BF16)
    two1 = (two_own, swap(two_own, "col", 1))
    active1, slope1, final_send, final_mine = mlp_forward(*two1, up1, down1, up_bias1)

    gains = (params[0][0], params[0][2], params[1][0], params[1][2])
    weights = (attend1, up1, down1)
    saved = (resid1, one1, qkv1, context1, middle1, two1, active1, slope1)
    chip, arrived, parts, hidden_sum1, mlp_sum1 = mlp_part(ends, saved, weights)
    two, ends, grad_hidden, active = parts
    grads = weight_grads([(two, grad_hidden)], [(ends, active)], "mlp_grad")
    second_ring_x, second_ring_z = Ring("x", *grads[:5]), Ring("z", *grads[5:])
    final_send, final_mine, _ = lax.optimization_barrier((final_send, final_mine, chip))
    final_chip = chip_sum(final_send, final_mine)
    marks = (second_ring_x.low, second_ring_x.high, second_ring_z.low, second_ring_z.high)
    arrived = after(arrived, *grads, final_chip, *marks)
    own, two_sums1, grad_middle = norm_backward(chip, arrived, middle1, gains[3], ends[0], True)
    pair = (own, swap(own, "col", 1))

    chip, arrived, parts, qv_sum1, attend_sum1 = attend_part(pair, saved, weights, bias)
    attend_blocks = weight_grads(*parts, "attend_grad")
    second_x, second_z = second_ring_x.finish(chip), second_ring_z.finish(chip)
    one_sums1 = norm_sums(chip, resid1)
    arrived = after(
        arrived, *attend_blocks, one_sums1, *second_ring_x.sent, *second_ring_z.sent
    )
    grad_mid = norm_backward(chip, arrived, resid1, gains[2], grad_middle, False)[0]

    ends = (grad_mid, swap(grad_mid, "col", 1))
    weights = (attend0, up0, down0)
    saved = (resid0, one0, qkv0, context0, middle0, two0, active0, slope0)
    chip, arrived, parts, hidden_sum0, mlp_sum0 = mlp_part(ends, saved, weights)
    two, ends, grad_hidden, active = parts
    grads = weight_grads([(two, grad_hidden)], [(ends, active)], "mlp_grad", attend_blocks)
    ring_x, ring_z = Ring("x", *grads[:5]), Ring("z", *grads[5:])
    arrived = after(arrived, *grads, *second_x, *second_z)
    own, two_sums0, grad_middle = norm_backward(chip, arrived, middle0, gains[1], ends[0], True)
    pair = (own, swap(own, "col", 1))
    marks = (ring_x.low, ring_x.high, ring_z.low, ring_z.high)
    chip, arrived, parts, qv_sum0, attend_sum0 = attend_part(pair, saved, weights, bias, marks)
    sums = (norm_sums(chip, resid0), two_sums0, qv_sum0, hidden_sum0, attend_sum0, mlp_sum0)
    sums += (one_sums1, two_sums1, qv_sum1, hidden_sum1, attend_sum1, mlp_sum1)
    sums = call(pack_sums_kernel, [((16, D), F32)], sums, "pack_sums")
    grads = weight_grads(*parts, "attend_grad", ride=sums)
    attend_ring_x, attend_ring_z = Ring("x", *grads[:5]), Ring("z", *grads[5:])
    marks = (attend_ring_x.low, attend_ring_x.high, attend_ring_z.low, attend_ring_z.high)
    parts_x = ring_x.finish(*marks, beside=(attend_ring_x,), ride=sums)
    parts_z = ring_z.finish(*marks, beside=(attend_ring_z,))
    arrived = after(arrived, *ring_x.sent, *ring_z.sent)
    input_own = norm_backward(chip, arrived, resid0, gains[0], grad_middle, False)[0]

    input_grad = feature_block(input_own)
    parts_x = lax.optimization_barrier((*parts_x, input_grad))[:3]
    parts_z = lax.optimization_barrier((*parts_z, input_grad))[:3]
    light_x = light_ring("x", parts_x, second_x, ride=ring_x.ride)
    light_z = light_ring("z", parts_z, second_z)
    marks = (light_x.low, light_x.high, light_z.low, light_z.high)
    total_x, sums = light_sum(light_x, *marks)
    total_z = light_sum(light_z, *marks)

    final_chip = after(final_chip, *ring_x.sent, *ring_z.sent)
    final_arrived = swap(final_chip, "col", 2)
    final_chip = after(final_chip, total_z)
    final = middle1 + col_sum(final_chip, final_arrived) + down_bias1
    final = feature_block(final.astype(BF16))
    total_x = after(total_x, final)
    def for_sections(first, second):
        sent = jnp.where(leading, second, first).astype(BF16)
        return jnp.where(leading, first, second), sent

    mine, sent = for_sections(
        jnp.concatenate([total_x[:, :1024], total_z[:, :1024]], 1),
        jnp.concatenate([total_x[:, 2048:], total_z[:, 2048:]], 1),
    )
    total_mlp = mine + swap(sent, "section", 1).astype(F32)
    mine, sent = for_sections(
        jnp.concatenate([total_x[:, 1536:2048], total_z[:, 1536:2048]], 1),
        jnp.concatenate([total_x[:, 1024:1536], total_z[:, 1024:1536]], 1),
    )
    sums, sums_sent = for_sections(sums[:8], sums[8:])
    arrived = swap(jnp.concatenate([sent, sums_sent, sums_sent], 0), "section", 1).astype(F32)
    total_attend = mine + arrived[:64]
    sums = sums + arrived[64:72]
    total_qkv = total_attend[:, :768].reshape(64, 3, 256)
    total_vo = total_attend[:, 768:]
    total_up, total_down = total_mlp[:, :1024], total_mlp[:, 1024:]

    outs = [((1, 256), F32)] * 6 + [((1, 2, 256), F32), ((1, 1024), F32)]
    halves = sums[:4] + swap(sums[:4], "col", 1)
    small = call(small_kernel, outs, (sums, halves, swap(halves[:2], "col", 2)), "small_outputs")

    return (
        final[None, None],
        input_grad[None, None],
        small[0],
        small[1],
        total_qkv[None],
        small[6],
        total_vo.T[None],
        small[4],
        small[2],
        small[3],
        total_up[None],
        small[7],
        total_down.T[None],
        small[5],
    )


def solution(mesh):
    placed = (
        P("section", "row", None, "col"),
        P("section", "row", None, "col"),
        P("section", "col"),
        P("section", "col"),
        P("section", "row", None, "col"),
        P("section", None, "col"),
        P("section", "col", "row"),
        P("section", "col"),
        P("section", "col"),
        P("section", "col"),
        P("section", "row", "col"),
        P("section", "col"),
        P("section", "col", "row"),
        P("section", "col"),
    )
    return jax.shard_map(
        local,
        mesh=mesh,
        in_specs=placed,
        out_specs=placed,
        check_vma=False,
    )
```
